32 devices in a mesh: freq: 2 (over y), sub: 16 (over z, x, core).
Axes of the slice: x: 2, y: 2, z: 4, core: 2. Of those that a mesh axis runs over, the one named last changes fastest.
Arguments:
- tri_xyz: float32 [3, 8192], P(None, 'sub'), may hold values from -1 to 1
- leaf_tri: int32 [32, 256], P('sub'), may hold values from 0 to 511, as said below
- leaf_proxy: int32 [32, 1024], P('sub'), may hold values from 0 to 8191
- node_proxy: int32 [16, 1024], P('sub'), may hold values from 0 to 8191
- mid_proxy: int32 [2, 1024], replicated, may hold values from 0 to 8191
- root_proxy: int32 [1024], replicated, may hold values from 0 to 8191
- level1_pos: int32 [16], P('sub'), may hold values from 0 to 7, as said below
- kappa: float32 [2], P('freq'), parts along dimension 0, may hold values from 20 to 40
- omega: float32 [2048, 128], replicated, may hold values from -0.125 to 0.125
Outputs:
- leaf_basis: float32 [64, 256, 128], P(('freq', 'sub')), parts along dimension 0
- node_transfer: float32 [32, 256, 128], P(('freq', 'sub')), parts along dimension 0
- mid_transfer: float32 [32, 128, 128], P(('freq', 'sub')), parts along dimension 0
- root_transfer: float32 [32, 16, 128], P(('freq', 'sub')), parts along dimension 0
The draws below stay inside these ranges and needn't reach their ends.
There are 2 independent parts, one for each index of `freq`. The reference program is written for one: setup_inputs(seed, part) draws one part's arguments, and reference() takes and returns one part's arrays. A program takes and returns all parts, laid end to end along the dimension named above; an argument that names none is the same for every part. Nothing has to cross between parts.
Inputs may be any that keep to these rules, and one draw needn't show every extreme that they name: `leaf_tri`: the 2 leaves of one level-one cluster name each of its 512 triangles once. `level1_pos`: each aligned block of 8 entries is a permutation.
All inputs are finite; a program needn't handle non-finite values.
Results may differ from the reference program's by a relative error of at most 0.04.
Values sent between devices are 32-bit elements; how exact they have to be, the bound alone decides.
A program may use at most 128 MiB of HBM per device.

```python
import jax
import jax.numpy as jnp
from jax import lax

LEAF_DEV = 2
LEAF_ROWS = 256
PROXY = 1024
RANK = 128
GROUP = 8
TRI_DEV = 512
TRIS = 8192
LEAVES = 32
MIDS = 2
SHARE = 16
N_SUB = 16


def draw_leaf_tri(key, part):
    key = jax.random.fold_in(key, 11)
    keys = jax.random.split(key, N_SUB)
    orders = jax.vmap(lambda single: jax.random.permutation(single, TRI_DEV))(keys)
    return orders.reshape(LEAVES, LEAF_ROWS).astype(jnp.int32)


def draw_level1_pos(key, part):
    key = jax.random.fold_in(key, 23)
    keys = jax.random.split(key, N_SUB // GROUP)
    orders = jax.vmap(lambda single: jax.random.permutation(single, GROUP))(keys)
    return orders.reshape(N_SUB).astype(jnp.int32)


def set_ends(entries, key, low, high):
    spot = [jax.random.randint(jax.random.fold_in(key, axis), (), 0, length) for axis, length in enumerate(entries.shape)]
    widest = entries.shape.index(max(entries.shape))
    beside = spot[:widest] + [(spot[widest] + 1) % entries.shape[widest]] + spot[widest + 1:]
    return entries.at[tuple(spot)].set(low).at[tuple(beside)].set(high)


def block_levels(stream_key, extent, shards, low, top_value):
    def one(position, shards_of):
        draws = jax.random.uniform(jax.random.fold_in(jax.random.fold_in(stream_key, 6), position), (shards_of,), jnp.float32, low / len(shards), top_value / len(shards))
        return jnp.repeat(jnp.exp(draws), extent[position] // shards_of).reshape((-1,) + (1,) * (len(extent) - position - 1))

    level = one(*shards[0])
    for cut in shards[1:]:
        level = level * one(*cut)
    return level


def gaussian(own_key, extent, deviation, reach, kind=jnp.bfloat16):
    drawn = jax.random.normal(own_key, extent, jnp.float32) * deviation
    return jnp.minimum(jnp.maximum(drawn, -reach), reach).astype(kind)


def setup_inputs(seed: int = 0, part: int = 0) -> dict:
    key_of = jax.random.split(jax.random.key(seed), 10)
    part_keys = jax.random.split(jax.random.fold_in(key_of[9], part), 10)
    tri_xyz = jnp.clip(jax.random.uniform(key_of[0], (3, TRIS), jnp.float32, -1.0, 1.0) * block_levels(key_of[0], (3, TRIS), ((1, 16),), -0.4, 0.0), -1.0, 1.0)
    leaf_tri = draw_leaf_tri(jax.random.fold_in(key_of[9], 71), part)
    leaf_proxy = set_ends(jax.random.randint(key_of[2], (LEAVES, PROXY), 0, TRIS), jax.random.fold_in(key_of[2], 1), 0, TRIS - 1).astype(jnp.int32)
    node_proxy = set_ends(jax.random.randint(key_of[3], (N_SUB, PROXY), 0, TRIS), jax.random.fold_in(key_of[3], 1), 0, TRIS - 1).astype(jnp.int32)
    mid_proxy = set_ends(jax.random.randint(key_of[4], (MIDS, PROXY), 0, TRIS), jax.random.fold_in(key_of[4], 1), 0, TRIS - 1).astype(jnp.int32)
    root_proxy = set_ends(jax.random.randint(key_of[5], (PROXY,), 0, TRIS), jax.random.fold_in(key_of[5], 1), 0, TRIS - 1).astype(jnp.int32)
    level1_pos = draw_level1_pos(jax.random.fold_in(key_of[9], 71), part)
    kappa = jnp.clip(jax.random.uniform(part_keys[7], (1,), jnp.float32, 20.0, 40.0), 20.0, 40.0)
    omega = gaussian(key_of[8], (2 * PROXY, RANK), (2 * PROXY) ** -0.5, 0.125, jnp.float32)
    return {"tri_xyz": tri_xyz, "leaf_tri": leaf_tri, "leaf_proxy": leaf_proxy, "node_proxy": node_proxy, "mid_proxy": mid_proxy, "root_proxy": root_proxy, "level1_pos": level1_pos, "kappa": kappa, "omega": omega}


soft_sq = 0.0025

def samples(rows_xyz, cols_xyz, wavenum):
    first = rows_xyz[0][:, None] - cols_xyz[0][None, :]
    squared = first * first
    second = rows_xyz[1][:, None] - cols_xyz[1][None, :]
    squared = squared + second * second
    third = rows_xyz[2][:, None] - cols_xyz[2][None, :]
    squared = squared + third * third
    distance = jnp.sqrt(squared + soft_sq)
    phases = wavenum * distance
    return jnp.concatenate([jnp.cos(phases) / distance, jnp.sin(phases) / distance], axis=1)

def sketch(rows_xyz, cols_xyz, wavenum, omega):
    return jnp.dot(samples(rows_xyz, cols_xyz, wavenum).astype(jnp.float32), omega.astype(jnp.float32), precision=lax.Precision.HIGHEST, preferred_element_type=jnp.float32)

def orthonormal(sketch_in):
    gram_matrix = jnp.dot(sketch_in.T, sketch_in, precision=lax.Precision.HIGHEST)
    factor = jnp.linalg.cholesky(gram_matrix)
    return lax.linalg.triangular_solve(factor, sketch_in, left_side=False, lower=True, transpose_a=True)

def reference(tri_xyz, leaf_tri, leaf_proxy, node_proxy, mid_proxy, root_proxy, level1_pos, kappa, omega):
    wavenum = kappa[0]
    highest = lax.Precision.HIGHEST

    def leaf_work(leaf_index):
        owner_dev = leaf_index // LEAF_DEV
        tri_cols = leaf_tri[leaf_index] + owner_dev * TRI_DEV
        rows_xyz = jnp.take(tri_xyz, tri_cols, axis=1)
        own_sketch = sketch(rows_xyz, jnp.take(tri_xyz, leaf_proxy[leaf_index], axis=1), wavenum, omega)
        basis = orthonormal(own_sketch)
        upward = []
        for proxies in (node_proxy[owner_dev], mid_proxy[owner_dev // GROUP], root_proxy):
            far_samples = sketch(rows_xyz, jnp.take(tri_xyz, proxies, axis=1), wavenum, omega)
            upward.append(jnp.dot(basis.T, far_samples, precision=highest))
        return (basis, upward[0], upward[1], upward[2])
    leaf_basis, level_one, second, level_three = lax.map(leaf_work, jnp.arange(LEAVES, dtype=jnp.int32))

    def node_work(stacks):
        transfer = orthonormal(stacks[0].reshape(-1, RANK))
        coef_two = jnp.dot(transfer.T, stacks[1].reshape(-1, RANK), precision=highest)
        coef_three = jnp.dot(transfer.T, stacks[2].reshape(-1, RANK), precision=highest)
        return (transfer, coef_two, coef_three)
    shaped = (level_one.reshape(N_SUB, LEAF_DEV, RANK, RANK), second.reshape(N_SUB, LEAF_DEV, RANK, RANK), level_three.reshape(N_SUB, LEAF_DEV, RANK, RANK))
    node_transfer, coef_two, coef_three = lax.map(node_work, shaped)
    place_one = (level1_pos.reshape(MIDS, GROUP)[:, :, None] == jnp.arange(GROUP, dtype=jnp.int32)[None, None, :]).astype(jnp.float32)
    stack_two = jnp.einsum('gcs,gcij->gsij', place_one, coef_two.reshape(MIDS, GROUP, RANK, RANK), precision=highest)
    stack_three = jnp.einsum('gcs,gcij->gsij', place_one, coef_three.reshape(MIDS, GROUP, RANK, RANK), precision=highest)

    def mid_work(stacks):
        transfer = orthonormal(stacks[0].reshape(GROUP * RANK, RANK))
        return (transfer, jnp.dot(transfer.T, stacks[1].reshape(GROUP * RANK, RANK), precision=highest))
    mid_full, coef_root = lax.map(mid_work, (stack_two, stack_three))
    mid_blocks = mid_full.reshape(MIDS, GROUP, RANK, RANK)
    mid_transfer = jnp.einsum('gcs,gsij->gcij', place_one, mid_blocks, precision=highest).reshape(N_SUB, RANK, RANK)
    stack_root = coef_root.reshape(MIDS * RANK, RANK)
    root_full = orthonormal(stack_root).reshape(MIDS, GROUP, SHARE, RANK)
    root_transfer = jnp.einsum('gcs,gskj->gckj', place_one, root_full, precision=highest).reshape(N_SUB, SHARE, RANK)
    return (leaf_basis, node_transfer, mid_transfer, root_transfer)
```

```python
import functools
import math

import jax
import jax.numpy as jnp
from jax import lax
from jax.experimental import pallas as pl
from jax.experimental.pallas import tpu as pltpu
from jax.sharding import PartitionSpec as P

GROUP = 8
LANES = 128
ROWS8 = 8
ROW_CHUNK = 128
soft_sq = 0.0025
MESH = pl.DeviceIdType.MESH
F32 = jnp.float32
BF16 = jnp.bfloat16

SIN_COEF = (
    3.141592640130707,
    -5.167710083507899,
    2.5500775232144695,
    -0.5982912856189484,
    0.07765766030176967,
)
COS_COEF = (
    1.9999999064952165,
    -9.8695856612393,
    8.116822705725152,
    -2.6637531361606688,
    0.43937922219243786,
)


def split(block):
    high = block.astype(BF16)
    return high, (block - high.astype(F32)).astype(BF16)


def dot3(left, right, dims):
    left_high, left_low = split(left)
    right_high, right_low = split(right)
    dot = functools.partial(
        lax.dot_general, dimension_numbers=(dims, ((), ())), preferred_element_type=F32
    )
    return dot(left_high, right_high) + (dot(left_high, right_low) + dot(left_low, right_high))


def mul_nn(left, right):
    return dot3(left, right, ((1,), (0,)))


def mul_nt(left, right):
    return dot3(left, right, ((1,), (1,)))


def mul_tn(left, right):
    return dot3(left, right, ((0,), (0,)))


def inverse_factors(grams):
    size = grams[0].shape[0]
    lane = lax.broadcasted_iota(jnp.int32, (ROWS8, size), 1)
    sub = lax.broadcasted_iota(jnp.int32, (ROWS8, size), 0)
    states = list(grams)
    done = [[] for _ in grams]
    for start in range(0, size, ROWS8):
        stop = start + ROWS8
        in_panel = (lane >= start) & (lane < stop)
        unit = (lane - start == sub).astype(F32)
        for which, state in enumerate(states):
            panel = state[:ROWS8]
            entry = {}
            for col in range(ROWS8):
                column = jnp.broadcast_to(panel[:, start + col : start + col + 1], (ROWS8, size))
                for row in range(col, ROWS8):
                    entry[row, col] = jnp.broadcast_to(column[row : row + 1], (ROWS8, size))
            right = jnp.where(in_panel, unit, panel)
            lines = [jnp.broadcast_to(right[row : row + 1], (ROWS8, size)) for row in range(ROWS8)]
            for k in range(ROWS8):
                scale = lax.rsqrt(entry[k, k])
                lines[k] = lines[k] * scale
                for row in range(k + 1, ROWS8):
                    entry[row, k] = entry[row, k] * scale
                for row in range(k + 1, ROWS8):
                    lines[row] = lines[row] - entry[row, k] * lines[k]
                    for col in range(k + 1, row + 1):
                        entry[row, col] = entry[row, col] - entry[row, k] * entry[col, k]
            solved = lines[0]
            for k in range(1, ROWS8):
                solved = jnp.where(sub == k, lines[k], solved)
            done[which].append(jnp.where(lane < stop, solved, 0.0))
            if stop < size:
                high, low = split(solved)
                high_f, low_f = high.astype(F32), low.astype(F32)
                left = jnp.concatenate([high_f, low_f, high_f, jnp.zeros_like(high_f)], axis=0)
                right = jnp.concatenate([high_f, high_f, low_f, jnp.zeros_like(high_f)], axis=0)
                update = lax.dot_general(
                    left.T[stop:].astype(BF16),
                    right.astype(BF16),
                    (((1,), (0,)), ((), ())),
                    preferred_element_type=F32,
                )
                rest = state[ROWS8:]
                rest_lane = lax.broadcasted_iota(jnp.int32, rest.shape, 1)
                rest = jnp.where((rest_lane >= start) & (rest_lane < stop), 0.0, rest)
                states[which] = rest - update
    return [jnp.concatenate(rows, axis=0) for rows in done]


def gather_kernel(count, own_ref, table_ref, send_sem, recv_sem, local_sem):
    me = lax.axis_index("sub")
    barrier = pltpu.get_barrier_semaphore()

    def greet(step, carry):
        pl.semaphore_signal(
            barrier, inc=1, device_id={"sub": lax.rem(me + step, count)}, device_id_type=MESH
        )
        return carry

    lax.fori_loop(1, count, greet, 0)
    local = pltpu.make_async_copy(own_ref, table_ref.at[:, me], local_sem)
    local.start()
    pl.semaphore_wait(barrier, count - 1)

    def copy_of(step):
        return pltpu.make_async_remote_copy(
            src_ref=own_ref,
            dst_ref=table_ref.at[:, me],
            send_sem=send_sem.at[step],
            recv_sem=recv_sem.at[step],
            device_id={"sub": lax.rem(me + step, count)},
            device_id_type=MESH,
        )

    def start(step, carry):
        copy_of(step).start()
        return carry

    def finish(step, carry):
        copy_of(step).wait()
        return carry

    lax.fori_loop(1, count, start, 0)
    local.wait()
    lax.fori_loop(1, count, finish, 0)


def leaf_kernel(
    per_dev,
    kappa_ref,
    table_ref,
    leaf_tri_ref,
    leaf_proxy_ref,
    node_proxy_ref,
    mid_proxy_ref,
    root_proxy_ref,
    omega_ref,
    basis_ref,
    transfer_ref,
    coef_ref,
    sums_ref,
    cols_ref,
    rows_ref,
    weight_ref,
    high_ref,
    low_ref,
    sketch_ref,
):
    device = lax.axis_index("sub")
    leaves, leaf_rows = leaf_tri_ref.shape
    proxies = leaf_proxy_ref.shape[1]
    rank = omega_ref.shape[1]
    rows = leaves * leaf_rows

    pieces = []
    for axis in range(3):
        turned = table_ref[axis].T
        first = turned.astype(BF16)
        left = turned - first.astype(F32)
        second = left.astype(BF16)
        third = (left - second.astype(F32)).astype(BF16)
        pieces.append((first, second, third))
    blocks = table_ref.shape[1]

    def centroids(index):
        width = index.shape[1]
        within = index % per_dev
        block = (index // per_dev) * ROWS8 + within // LANES
        place = within % LANES
        hot = jnp.where(
            lax.broadcasted_iota(jnp.int32, (blocks, width), 0) == block, 1.0, 0.0
        ).astype(BF16)
        chosen = lax.broadcasted_iota(jnp.int32, (LANES, width), 0) == place
        found = []
        for axis in range(3):
            wide = None
            for piece in pieces[axis]:
                term = jnp.dot(piece, hot, preferred_element_type=F32)
                wide = term if wide is None else wide + term
            found.append(jnp.sum(jnp.where(chosen, wide, 0.0), axis=0, keepdims=True))
        return found

    group = device // GROUP
    sets = [leaf_proxy_ref[leaf : leaf + 1, :] for leaf in range(leaves)]
    sets += [node_proxy_ref[...], mid_proxy_ref[pl.ds(group, 1), :], root_proxy_ref[...]]
    for number, index in enumerate(sets):
        found = centroids(index)
        for axis in range(3):
            cols_ref[number, axis : axis + 1, :] = found[axis]
    for leaf in range(leaves):
        found = centroids(leaf_tri_ref[leaf : leaf + 1, :] + device * per_dev)
        turned = jnp.concatenate(found + [jnp.zeros((ROWS8 - 3, leaf_rows), F32)], axis=0).T
        for axis in range(3):
            rows_ref[axis, leaf * leaf_rows : (leaf + 1) * leaf_rows, :] = jnp.broadcast_to(
                turned[:, axis : axis + 1], (leaf_rows, rows_ref.shape[2])
            )

    omega_high, omega_low = split(omega_ref[...])
    weight_ref[:, :rank] = omega_high
    weight_ref[:, rank:] = omega_low

    turns = kappa_ref[0] * (0.5 / math.pi)
    chunks = rows // ROW_CHUNK
    per_leaf = leaf_rows // ROW_CHUNK
    width = rows_ref.shape[2]

    def poly(coef, value):
        total = jnp.full_like(value, coef[-1])
        for number in coef[-2::-1]:
            total = total * value + number
        return total

    def sketches(step, carry):
        level = step // chunks
        chunk = step % chunks
        number = jnp.where(level == 0, chunk // per_leaf, level + leaves - 1)
        base = pl.multiple_of(chunk * ROW_CHUNK, ROW_CHUNK)
        for top in range(0, ROW_CHUNK, 16):
            mine = [rows_ref[axis, pl.ds(base + top, 16), :] for axis in range(3)]
            for begin in range(0, proxies, width):
                squared = None
                for axis in range(3):
                    apart = mine[axis] - cols_ref[number, axis : axis + 1, begin : begin + width]
                    squared = apart * apart if squared is None else squared + apart * apart
                squared = squared + soft_sq
                inverse = lax.rsqrt(squared)
                phase = (squared * inverse) * turns
                phase = phase - jnp.round(phase)
                square = phase * phase
                sine = phase * poly(SIN_COEF, square)
                twice = poly(COS_COEF, square)
                imag = (sine * twice) * inverse
                sine = sine * sine
                real = (1.0 - (sine + sine)) * inverse
                for value, offset in ((real, 0), (imag, proxies)):
                    high, low = split(value)
                    high_ref[top : top + 16, offset + begin : offset + begin + width] = high
                    low_ref[top : top + 16, offset + begin : offset + begin + width] = low
        wide = jnp.dot(high_ref[...], weight_ref[...], preferred_element_type=F32)
        fine = jnp.dot(low_ref[...], weight_ref[:, :rank], preferred_element_type=F32)
        sketch_ref[level, pl.ds(base, ROW_CHUNK), :] = wide[:, :rank] + (wide[:, rank:] + fine)
        return carry

    lax.fori_loop(0, 4 * chunks, sketches, 0)

    own = [sketch_ref[0, leaf * leaf_rows : (leaf + 1) * leaf_rows, :] for leaf in range(leaves)]
    factors = inverse_factors([mul_tn(block, block) for block in own])
    upward = []
    for leaf in range(leaves):
        basis = mul_nt(own[leaf], factors[leaf])
        basis_ref[leaf] = basis
        far = jnp.concatenate(
            [sketch_ref[k, leaf * leaf_rows : (leaf + 1) * leaf_rows, :] for k in (1, 2, 3)], axis=1
        )
        upward.append(mul_tn(basis, far))
    stacked = jnp.concatenate(upward, axis=0)
    first = stacked[:, :rank]
    (factor,) = inverse_factors([mul_tn(first, first)])
    transfer = mul_nt(first, factor)
    transfer_ref[...] = transfer
    coefs = mul_tn(transfer, stacked[:, rank:])
    coef_ref[...] = coefs[:, :rank]
    sums = mul_tn(coefs[:, :rank], coefs)
    sums_ref[:rank] = sums[:, :rank]
    sums_ref[rank:] = sums[:, rank:]


def tree_kernel(
    mids,
    pos_ref,
    coef_ref,
    sums_ref,
    mid_ref,
    root_ref,
    part_ref,
    full_ref,
    own_ref,
    other_ref,
    part_send,
    part_recv,
    full_send,
    full_recv,
    root_send,
    root_recv,
):
    rank = coef_ref.shape[0]
    count = mids * GROUP
    me = lax.axis_index("sub")
    member = lax.rem(me, GROUP)
    first = me - member
    share = sums_ref.shape[0] // GROUP

    def sibling(step):
        return first + lax.rem(member + step, GROUP)

    def cousin(step):
        return lax.rem(me + step * GROUP, count)

    barrier = pltpu.get_barrier_semaphore()
    for step in range(1, GROUP):
        pl.semaphore_signal(
            barrier, inc=1, device_id={"sub": sibling(step)}, device_id_type=MESH
        )
    for step in range(1, mids):
        pl.semaphore_signal(barrier, inc=1, device_id={"sub": cousin(step)}, device_id_type=MESH)
    pl.semaphore_wait(barrier, GROUP - 1 + mids - 1)

    copies = []
    for step in range(1, GROUP):
        begin = pl.multiple_of(lax.rem(member + step, GROUP) * share, share)
        copy = pltpu.make_async_remote_copy(
            src_ref=sums_ref.at[pl.ds(begin, share)],
            dst_ref=part_ref.at[step],
            send_sem=part_send.at[step],
            recv_sem=part_recv.at[step],
            device_id={"sub": sibling(step)},
            device_id_type=MESH,
        )
        copy.start()
        copies.append(copy)
    begin = pl.multiple_of(member * share, share)
    total = sums_ref[pl.ds(begin, share), :]
    for step, copy in enumerate(copies, 1):
        copy.wait()
        total = total + part_ref[step]
    full_ref[pl.ds(begin, share), :] = total
    copies = []
    for step in range(1, GROUP):
        copy = pltpu.make_async_remote_copy(
            src_ref=full_ref.at[pl.ds(begin, share)],
            dst_ref=full_ref.at[pl.ds(begin, share)],
            send_sem=full_send.at[step],
            recv_sem=full_recv.at[step],
            device_id={"sub": sibling(step)},
            device_id_type=MESH,
        )
        copy.start()
        copies.append(copy)
    for copy in copies:
        copy.wait()

    (factor,) = inverse_factors([full_ref[:rank]])
    own = mul_nn(factor, full_ref[rank:])
    own_ref[...] = own
    copies = []
    for step in range(1, mids):
        copy = pltpu.make_async_remote_copy(
            src_ref=own_ref,
            dst_ref=other_ref.at[step],
            send_sem=root_send.at[step],
            recv_sem=root_recv.at[step],
            device_id={"sub": cousin(step)},
            device_id_type=MESH,
        )
        copy.start()
        copies.append(copy)
    mid_ref[...] = mul_nt(coef_ref[...], factor)
    gram = mul_tn(own, own)
    for step, copy in enumerate(copies, 1):
        copy.wait()
        other = other_ref[step]
        gram = gram + mul_tn(other, other)
    (factor,) = inverse_factors([gram])
    share_rows = rank // GROUP
    mine = jnp.zeros((share_rows, rank), F32)
    for place in range(GROUP):
        block = own[place * share_rows : (place + 1) * share_rows]
        mine = jnp.where(pos_ref[...] == place, block, mine)
    root_ref[...] = mul_nt(mine, factor)


def on_device(
    tri_xyz, leaf_tri, leaf_proxy, node_proxy, mid_proxy, root_proxy, level1_pos, kappa, omega
):
    count = lax.axis_size("sub")
    mids = count // GROUP
    per_dev = tri_xyz.shape[1]
    leaves, leaf_rows = leaf_tri.shape
    proxies = leaf_proxy.shape[1]
    rank = omega.shape[1]
    vmem = pl.BlockSpec(memory_space=pltpu.VMEM)
    smem = pl.BlockSpec(memory_space=pltpu.SMEM)
    dma = pltpu.SemaphoreType.DMA
    limit = 48 * 1024 * 1024

    own = tri_xyz.reshape(3, per_dev // LANES, LANES)
    own = jnp.pad(own, ((0, 0), (0, ROWS8 - per_dev // LANES), (0, 0)))
    table = pl.pallas_call(
        functools.partial(gather_kernel, count),
        out_shape=jax.ShapeDtypeStruct((3, count, ROWS8, LANES), F32),
        in_specs=[vmem],
        out_specs=vmem,
        scratch_shapes=[dma((count,)), dma((count,)), dma],
        compiler_params=pltpu.CompilerParams(
            collective_id=0, has_side_effects=True, vmem_limit_bytes=limit
        ),
        name="gather_centroids",
    )(own)
    table = table.reshape(3, count * ROWS8, LANES)

    basis, transfer, coef, sums = pl.pallas_call(
        functools.partial(leaf_kernel, per_dev),
        out_shape=(
            jax.ShapeDtypeStruct((leaves, leaf_rows, rank), F32),
            jax.ShapeDtypeStruct((leaves * rank, rank), F32),
            jax.ShapeDtypeStruct((rank, rank), F32),
            jax.ShapeDtypeStruct((2 * rank, rank), F32),
        ),
        in_specs=[smem] + [vmem] * 7,
        out_specs=(vmem,) * 4,
        scratch_shapes=[
            pltpu.VMEM((leaves + 3, ROWS8, proxies), F32),
            pltpu.VMEM((3, leaves * leaf_rows, 2 * LANES), F32),
            pltpu.VMEM((2 * proxies, 2 * rank), BF16),
            pltpu.VMEM((ROW_CHUNK, 2 * proxies), BF16),
            pltpu.VMEM((ROW_CHUNK, 2 * proxies), BF16),
            pltpu.VMEM((4, leaves * leaf_rows, rank), F32),
        ],
        compiler_params=pltpu.CompilerParams(vmem_limit_bytes=limit),
        name="leaf_and_node",
    )(kappa, table, leaf_tri, leaf_proxy, node_proxy, mid_proxy, root_proxy[None], omega)

    share = 2 * rank // GROUP
    mid, root = pl.pallas_call(
        functools.partial(tree_kernel, mids),
        out_shape=(
            jax.ShapeDtypeStruct((rank, rank), F32),
            jax.ShapeDtypeStruct((rank // GROUP, rank), F32),
        ),
        in_specs=[vmem, vmem, vmem],
        out_specs=(vmem, vmem),
        scratch_shapes=[
            pltpu.VMEM((GROUP, share, rank), F32),
            pltpu.VMEM((2 * rank, rank), F32),
            pltpu.VMEM((rank, rank), F32),
            pltpu.VMEM((mids, rank, rank), F32),
            dma((GROUP,)),
            dma((GROUP,)),
            dma((GROUP,)),
            dma((GROUP,)),
            dma((mids,)),
            dma((mids,)),
        ],
        compiler_params=pltpu.CompilerParams(
            collective_id=1, has_side_effects=True, vmem_limit_bytes=limit
        ),
        name="mid_and_root",
    )(jnp.broadcast_to(level1_pos[0], (rank // GROUP, rank)), coef, sums)
    return (basis, transfer[None], mid[None], root[None])


def solution(mesh):
    in_specs = (
        P(None, "sub"),
        P("sub", None),
        P("sub", None),
        P("sub", None),
        P(),
        P(),
        P("sub"),
        P("freq"),
        P(),
    )
    out_specs = (
        P(("freq", "sub"), None, None),
        P(("freq", "sub"), None, None),
        P(("freq", "sub"), None, None),
        P(("freq", "sub"), None, None),
    )
    return jax.shard_map(
        on_device, mesh=mesh, in_specs=in_specs, out_specs=out_specs, check_vma=False
    )
```

```python
import functools
import math

import jax
import jax.numpy as jnp
from jax import lax
from jax.experimental import pallas as pl
from jax.experimental.pallas import tpu as pltpu
from jax.sharding import PartitionSpec as P

GROUP = 8
LANES = 128
ROWS8 = 8
ROW_CHUNK = 128
soft_sq = 0.0025
MESH = pl.DeviceIdType.MESH
F32 = jnp.float32
BF16 = jnp.bfloat16

SIN_COEF = (
    3.141592640130707,
    -5.167710083507899,
    2.5500775232144695,
    -0.5982912856189484,
    0.07765766030176967,
)
COS_COEF = (
    1.9999999064952165,
    -9.8695856612393,
    8.116822705725152,
    -2.6637531361606688,
    0.43937922219243786,
)


def split(block):
    high = block.astype(BF16)
    return high, (block - high.astype(F32)).astype(BF16)


def dot3(left, right, dims):
    left_high, left_low = split(left)
    right_high, right_low = split(right)
    dot = functools.partial(
        lax.dot_general, dimension_numbers=(dims, ((), ())), preferred_element_type=F32
    )
    return dot(left_high, right_high) + (dot(left_high, right_low) + dot(left_low, right_high))


def mul_nn(left, right):
    return dot3(left, right, ((1,), (0,)))


def mul_nt(left, right):
    return dot3(left, right, ((1,), (1,)))


def mul_tn(left, right):
    return dot3(left, right, ((0,), (0,)))


def inverse_factors(grams, scratch):
    size = grams[0].shape[0]
    panels = size // ROWS8
    lane = lax.broadcasted_iota(jnp.int32, (ROWS8, size), 1)
    sub = lax.broadcasted_iota(jnp.int32, (ROWS8, size), 0)
    states = [[gram[p * ROWS8 : (p + 1) * ROWS8] for p in range(panels)] for gram in grams]
    done = [[] for _ in grams]

    def columns(block, start):
        return [
            jnp.broadcast_to(block[:, start + col : start + col + 1], (ROWS8, size))
            for col in range(ROWS8)
        ]

    for number in range(panels):
        start = number * ROWS8
        in_panel = (lane >= start) & (lane < start + ROWS8)
        unit = (lane - start == sub).astype(F32)
        for which, rows in enumerate(states):
            panel = rows[number]
            entry = {}
            slot = scratch.at[which, number % 2]
            for col, column in enumerate(columns(panel, start)):
                slot[col] = column
                for row in range(col, ROWS8):
                    entry[row, col] = jnp.broadcast_to(slot[col, row : row + 1], (ROWS8, size))
            slot[ROWS8] = jnp.where(in_panel, unit, panel)
            lines = [
                jnp.broadcast_to(slot[ROWS8, row : row + 1], (ROWS8, size)) for row in range(ROWS8)
            ]
            last = number + 1 == panels
            if not last:
                below = columns(rows[number + 1], start)
                later = jnp.where(in_panel, 0.0, rows[number + 1])
            for k in range(ROWS8):
                scale = lax.rsqrt(entry[k, k])
                lines[k] = lines[k] * scale
                for row in range(k + 1, ROWS8):
                    entry[row, k] = entry[row, k] * scale
                if not last:
                    below[k] = below[k] * scale
                    later = later - below[k] * lines[k]
                for row in range(k + 1, ROWS8):
                    factor = entry[row, k]
                    lines[row] = lines[row] - factor * lines[k]
                    if not last:
                        below[row] = below[row] - factor * below[k]
                    for col in range(k + 1, row + 1):
                        entry[row, col] = entry[row, col] - factor * entry[col, k]
            solved = lines[0]
            for k in range(1, ROWS8):
                solved = jnp.where(sub == k, lines[k], solved)
            done[which].append(jnp.where(lane < start + ROWS8, solved, 0.0))
            if not last:
                rows[number + 1] = later
            after = (number + 2) * ROWS8
            if after < size:
                high, low = split(solved)
                high_f, low_f = high.astype(F32), low.astype(F32)
                zero = jnp.zeros_like(high_f)
                left = jnp.concatenate([high_f, low_f, high_f, zero], axis=0).astype(BF16)
                right = jnp.concatenate([high_f, high_f, low_f, zero], axis=0).astype(BF16)
                update = lax.dot_general(
                    left, right, (((0,), (0,)), ((), ())), preferred_element_type=F32
                )[after:]
                for p in range(number + 2, panels):
                    begin = p * ROWS8 - after
                    rows[p] = jnp.where(in_panel, 0.0, rows[p]) - update[begin : begin + ROWS8]
    return [jnp.concatenate(rows, axis=0) for rows in done]


def gather_kernel(count, own_ref, table_ref, send_sem, recv_sem, local_sem):
    me = lax.axis_index("sub")
    barrier = pltpu.get_barrier_semaphore()

    def greet(step, carry):
        pl.semaphore_signal(
            barrier, inc=1, device_id={"sub": lax.rem(me + step, count)}, device_id_type=MESH
        )
        return carry

    lax.fori_loop(1, count, greet, 0)
    local = pltpu.make_async_copy(own_ref, table_ref.at[:, me], local_sem)
    local.start()
    pl.semaphore_wait(barrier, count - 1)

    def copy_of(step):
        return pltpu.make_async_remote_copy(
            src_ref=own_ref,
            dst_ref=table_ref.at[:, me],
            send_sem=send_sem.at[step],
            recv_sem=recv_sem.at[step],
            device_id={"sub": lax.rem(me + step, count)},
            device_id_type=MESH,
        )

    def start(step, carry):
        copy_of(step).start()
        return carry

    def finish(step, carry):
        copy_of(step).wait()
        return carry

    lax.fori_loop(1, count, start, 0)
    local.wait()
    lax.fori_loop(1, count, finish, 0)


def leaf_kernel(
    per_dev,
    kappa_ref,
    table_ref,
    leaf_tri_ref,
    leaf_proxy_ref,
    node_proxy_ref,
    mid_proxy_ref,
    root_proxy_ref,
    omega_ref,
    basis_ref,
    transfer_ref,
    coef_ref,
    sums_ref,
    cols_ref,
    rows_ref,
    weight_ref,
    high_ref,
    low_ref,
    high_too_ref,
    low_too_ref,
    sketch_ref,
    factor_ref,
):
    device = lax.axis_index("sub")
    leaves, leaf_rows = leaf_tri_ref.shape
    proxies = leaf_proxy_ref.shape[1]
    rank = omega_ref.shape[1]
    rows = leaves * leaf_rows

    pieces = []
    for axis in range(3):
        turned = table_ref[axis].T
        first = turned.astype(BF16)
        left = turned - first.astype(F32)
        second = left.astype(BF16)
        third = (left - second.astype(F32)).astype(BF16)
        pieces.append((first, second, third))
    blocks = table_ref.shape[1]

    def centroids(index):
        width = index.shape[1]
        within = index % per_dev
        block = (index // per_dev) * ROWS8 + within // LANES
        place = within % LANES
        hot = jnp.where(
            lax.broadcasted_iota(jnp.int32, (blocks, width), 0) == block, 1.0, 0.0
        ).astype(BF16)
        chosen = lax.broadcasted_iota(jnp.int32, (LANES, width), 0) == place
        found = []
        for axis in range(3):
            wide = None
            for piece in pieces[axis]:
                term = jnp.dot(piece, hot, preferred_element_type=F32)
                wide = term if wide is None else wide + term
            found.append(jnp.sum(jnp.where(chosen, wide, 0.0), axis=0, keepdims=True))
        return found

    group = device // GROUP
    sets = [leaf_proxy_ref[leaf : leaf + 1, :] for leaf in range(leaves)]
    sets += [node_proxy_ref[...], mid_proxy_ref[pl.ds(group, 1), :], root_proxy_ref[...]]
    for number, index in enumerate(sets):
        found = centroids(index)
        for axis in range(3):
            cols_ref[number, axis : axis + 1, :] = found[axis]
    for leaf in range(leaves):
        found = centroids(leaf_tri_ref[leaf : leaf + 1, :] + device * per_dev)
        turned = jnp.concatenate(found + [jnp.zeros((ROWS8 - 3, leaf_rows), F32)], axis=0).T
        for axis in range(3):
            rows_ref[axis, leaf * leaf_rows : (leaf + 1) * leaf_rows, :] = jnp.broadcast_to(
                turned[:, axis : axis + 1], (leaf_rows, rows_ref.shape[2])
            )

    omega_high, omega_low = split(omega_ref[...])
    weight_ref[:, :rank] = omega_high
    weight_ref[:, rank:] = omega_low

    turns = kappa_ref[0] * (0.5 / math.pi)
    chunks = rows // ROW_CHUNK
    per_leaf = leaf_rows // ROW_CHUNK
    width = rows_ref.shape[2]

    def poly(coef, value):
        total = jnp.full_like(value, coef[-1])
        for number in coef[-2::-1]:
            total = total * value + number
        return total

    def sample(step, slot):
        level = step // chunks
        chunk = step % chunks
        number = jnp.where(level == 0, chunk // per_leaf, level + leaves - 1)
        base = pl.multiple_of(chunk * ROW_CHUNK, ROW_CHUNK)
        for top in range(0, ROW_CHUNK, 16):
            mine = [rows_ref[axis, pl.ds(base + top, 16), :] for axis in range(3)]
            for begin in range(0, proxies, width):
                squared = None
                for axis in range(3):
                    apart = mine[axis] - cols_ref[number, axis : axis + 1, begin : begin + width]
                    squared = apart * apart if squared is None else squared + apart * apart
                squared = squared + soft_sq
                inverse = lax.rsqrt(squared)
                phase = (squared * inverse) * turns
                phase = phase - jnp.round(phase)
                square = phase * phase
                sine = phase * poly(SIN_COEF, square)
                twice = poly(COS_COEF, square)
                imag = (sine * twice) * inverse
                sine = sine * sine
                real = (1.0 - (sine + sine)) * inverse
                for value, offset in ((real, 0), (imag, proxies)):
                    high, low = split(value)
                    high_refs[slot][top : top + 16, offset + begin : offset + begin + width] = high
                    low_refs[slot][top : top + 16, offset + begin : offset + begin + width] = low

    def multiply(step, slot):
        base = pl.multiple_of((step % chunks) * ROW_CHUNK, ROW_CHUNK)
        wide = jnp.dot(high_refs[slot][...], weight_ref[...], preferred_element_type=F32)
        fine = jnp.dot(low_refs[slot][...], weight_ref[:, :rank], preferred_element_type=F32)
        sketch_ref[step // chunks, pl.ds(base, ROW_CHUNK), :] = wide[:, :rank] + (
            wide[:, rank:] + fine
        )

    high_refs = (high_ref, high_too_ref)
    low_refs = (low_ref, low_too_ref)
    steps = 4 * chunks
    sample(0, 0)

    def pair(half, carry):
        step = 2 * half
        multiply(step, 0)
        sample(step + 1, 1)
        multiply(step + 1, 1)
        sample(step + 2, 0)
        return carry

    lax.fori_loop(0, steps // 2 - 1, pair, 0)
    multiply(steps - 2, 0)
    sample(steps - 1, 1)
    multiply(steps - 1, 1)

    own = [sketch_ref[0, leaf * leaf_rows : (leaf + 1) * leaf_rows, :] for leaf in range(leaves)]
    factors = inverse_factors([mul_tn(block, block) for block in own], factor_ref)
    upward = []
    for leaf in range(leaves):
        basis = mul_nt(own[leaf], factors[leaf])
        basis_ref[leaf] = basis
        far = jnp.concatenate(
            [sketch_ref[k, leaf * leaf_rows : (leaf + 1) * leaf_rows, :] for k in (1, 2, 3)], axis=1
        )
        upward.append(mul_tn(basis, far))
    stacked = jnp.concatenate(upward, axis=0)
    first = stacked[:, :rank]
    (factor,) = inverse_factors([mul_tn(first, first)], factor_ref)
    transfer = mul_nt(first, factor)
    transfer_ref[...] = transfer
    coefs = mul_tn(transfer, stacked[:, rank:])
    coef_ref[...] = coefs[:, :rank]
    sums = mul_tn(coefs[:, :rank], coefs)
    sums_ref[:rank] = sums[:, :rank]
    sums_ref[rank:] = sums[:, rank:]


def tree_kernel(
    mids,
    pos_ref,
    coef_ref,
    sums_ref,
    mid_ref,
    root_ref,
    part_ref,
    full_ref,
    own_ref,
    other_ref,
    part_send,
    part_recv,
    full_send,
    full_recv,
    root_send,
    root_recv,
    factor_ref,
):
    rank = coef_ref.shape[0]
    count = mids * GROUP
    me = lax.axis_index("sub")
    member = lax.rem(me, GROUP)
    first = me - member
    share = sums_ref.shape[0] // GROUP

    def sibling(step):
        return first + lax.rem(member + step, GROUP)

    def cousin(step):
        return lax.rem(me + step * GROUP, count)

    barrier = pltpu.get_barrier_semaphore()
    for step in range(1, GROUP):
        pl.semaphore_signal(
            barrier, inc=1, device_id={"sub": sibling(step)}, device_id_type=MESH
        )
    for step in range(1, mids):
        pl.semaphore_signal(barrier, inc=1, device_id={"sub": cousin(step)}, device_id_type=MESH)
    pl.semaphore_wait(barrier, GROUP - 1 + mids - 1)

    copies = []
    for step in range(1, GROUP):
        begin = pl.multiple_of(lax.rem(member + step, GROUP) * share, share)
        copy = pltpu.make_async_remote_copy(
            src_ref=sums_ref.at[pl.ds(begin, share)],
            dst_ref=part_ref.at[step],
            send_sem=part_send.at[step],
            recv_sem=part_recv.at[step],
            device_id={"sub": sibling(step)},
            device_id_type=MESH,
        )
        copy.start()
        copies.append(copy)
    begin = pl.multiple_of(member * share, share)
    total = sums_ref[pl.ds(begin, share), :]
    for step, copy in enumerate(copies, 1):
        copy.wait()
        total = total + part_ref[step]
    full_ref[pl.ds(begin, share), :] = total
    copies = []
    for step in range(1, GROUP):
        copy = pltpu.make_async_remote_copy(
            src_ref=full_ref.at[pl.ds(begin, share)],
            dst_ref=full_ref.at[pl.ds(begin, share)],
            send_sem=full_send.at[step],
            recv_sem=full_recv.at[step],
            device_id={"sub": sibling(step)},
            device_id_type=MESH,
        )
        copy.start()
        copies.append(copy)
    for copy in copies:
        copy.wait()

    (factor,) = inverse_factors([full_ref[:rank]], factor_ref)
    own = mul_nn(factor, full_ref[rank:])
    own_ref[...] = own
    copies = []
    for step in range(1, mids):
        copy = pltpu.make_async_remote_copy(
            src_ref=own_ref,
            dst_ref=other_ref.at[step],
            send_sem=root_send.at[step],
            recv_sem=root_recv.at[step],
            device_id={"sub": cousin(step)},
            device_id_type=MESH,
        )
        copy.start()
        copies.append(copy)
    mid_ref[...] = mul_nt(coef_ref[...], factor)
    gram = mul_tn(own, own)
    for step, copy in enumerate(copies, 1):
        copy.wait()
        other = other_ref[step]
        gram = gram + mul_tn(other, other)
    (factor,) = inverse_factors([gram], factor_ref)
    share_rows = rank // GROUP
    mine = jnp.zeros((share_rows, rank), F32)
    for place in range(GROUP):
        block = own[place * share_rows : (place + 1) * share_rows]
        mine = jnp.where(pos_ref[...] == place, block, mine)
    root_ref[...] = mul_nt(mine, factor)


def on_device(
    tri_xyz, leaf_tri, leaf_proxy, node_proxy, mid_proxy, root_proxy, level1_pos, kappa, omega
):
    count = lax.axis_size("sub")
    mids = count // GROUP
    per_dev = tri_xyz.shape[1]
    leaves, leaf_rows = leaf_tri.shape
    proxies = leaf_proxy.shape[1]
    rank = omega.shape[1]
    vmem = pl.BlockSpec(memory_space=pltpu.VMEM)
    smem = pl.BlockSpec(memory_space=pltpu.SMEM)
    dma = pltpu.SemaphoreType.DMA
    limit = 48 * 1024 * 1024

    own = tri_xyz.reshape(3, per_dev // LANES, LANES)
    own = jnp.pad(own, ((0, 0), (0, ROWS8 - per_dev // LANES), (0, 0)))
    table = pl.pallas_call(
        functools.partial(gather_kernel, count),
        out_shape=jax.ShapeDtypeStruct((3, count, ROWS8, LANES), F32),
        in_specs=[vmem],
        out_specs=vmem,
        scratch_shapes=[dma((count,)), dma((count,)), dma],
        compiler_params=pltpu.CompilerParams(
            collective_id=0, has_side_effects=True, vmem_limit_bytes=limit
        ),
        name="gather_centroids",
    )(own)
    table = table.reshape(3, count * ROWS8, LANES)

    basis, transfer, coef, sums = pl.pallas_call(
        functools.partial(leaf_kernel, per_dev),
        out_shape=(
            jax.ShapeDtypeStruct((leaves, leaf_rows, rank), F32),
            jax.ShapeDtypeStruct((leaves * rank, rank), F32),
            jax.ShapeDtypeStruct((rank, rank), F32),
            jax.ShapeDtypeStruct((2 * rank, rank), F32),
        ),
        in_specs=[smem] + [vmem] * 7,
        out_specs=(vmem,) * 4,
        scratch_shapes=[
            pltpu.VMEM((leaves + 3, ROWS8, proxies), F32),
            pltpu.VMEM((3, leaves * leaf_rows, 2 * LANES), F32),
            pltpu.VMEM((2 * proxies, 2 * rank), BF16),
            pltpu.VMEM((ROW_CHUNK, 2 * proxies), BF16),
            pltpu.VMEM((ROW_CHUNK, 2 * proxies), BF16),
            pltpu.VMEM((ROW_CHUNK, 2 * proxies), BF16),
            pltpu.VMEM((ROW_CHUNK, 2 * proxies), BF16),
            pltpu.VMEM((4, leaves * leaf_rows, rank), F32),
            pltpu.VMEM((leaves, 2, ROWS8 + 1, ROWS8, rank), F32),
        ],
        compiler_params=pltpu.CompilerParams(vmem_limit_bytes=limit),
        name="leaf_and_node",
    )(kappa, table, leaf_tri, leaf_proxy, node_proxy, mid_proxy, root_proxy[None], omega)

    share = 2 * rank // GROUP
    mid, root = pl.pallas_call(
        functools.partial(tree_kernel, mids),
        out_shape=(
            jax.ShapeDtypeStruct((rank, rank), F32),
            jax.ShapeDtypeStruct((rank // GROUP, rank), F32),
        ),
        in_specs=[vmem, vmem, vmem],
        out_specs=(vmem, vmem),
        scratch_shapes=[
            pltpu.VMEM((GROUP, share, rank), F32),
            pltpu.VMEM((2 * rank, rank), F32),
            pltpu.VMEM((rank, rank), F32),
            pltpu.VMEM((mids, rank, rank), F32),
            dma((GROUP,)),
            dma((GROUP,)),
            dma((GROUP,)),
            dma((GROUP,)),
            dma((mids,)),
            dma((mids,)),
            pltpu.VMEM((1, 2, ROWS8 + 1, ROWS8, rank), F32),
        ],
        compiler_params=pltpu.CompilerParams(
            collective_id=1, has_side_effects=True, vmem_limit_bytes=limit
        ),
        name="mid_and_root",
    )(jnp.broadcast_to(level1_pos[0], (rank // GROUP, rank)), coef, sums)
    return (basis, transfer[None], mid[None], root[None])


def solution(mesh):
    in_specs = (
        P(None, "sub"),
        P("sub", None),
        P("sub", None),
        P("sub", None),
        P(),
        P(),
        P("sub"),
        P("freq"),
        P(),
    )
    out_specs = (
        P(("freq", "sub"), None, None),
        P(("freq", "sub"), None, None),
        P(("freq", "sub"), None, None),
        P(("freq", "sub"), None, None),
    )
    return jax.shard_map(
        on_device, mesh=mesh, in_specs=in_specs, out_specs=out_specs, check_vma=False
    )
```

```python
import functools
import math

import jax
import jax.numpy as jnp
from jax import lax
from jax.experimental import pallas as pl
from jax.experimental.pallas import tpu as pltpu
from jax.sharding import PartitionSpec as P

GROUP = 8
LANES = 128
ROWS8 = 8
ROW_CHUNK = 128
soft_sq = 0.0025
MESH = pl.DeviceIdType.MESH
F32 = jnp.float32
BF16 = jnp.bfloat16

SIN_COEF = (
    4.442882919124344,
    -7.30824568650907,
    3.606354218432694,
    -0.846111650371952,
    0.10982451642092537,
)
COS_COEF = (
    1.4142134962552284,
    -6.978850948563824,
    5.7394603769071955,
    -1.8835579059861416,
    0.31068802752474356,
)


def split(block):
    high = block.astype(BF16)
    return high, (block - high.astype(F32)).astype(BF16)


def dot3(left, right, dims):
    left_high, left_low = split(left)
    right_high, right_low = split(right)
    dot = functools.partial(
        lax.dot_general, dimension_numbers=(dims, ((), ())), preferred_element_type=F32
    )
    return dot(left_high, right_high) + (dot(left_high, right_low) + dot(left_low, right_high))


def mul_nn(left, right):
    return dot3(left, right, ((1,), (0,)))


def mul_nt(left, right):
    return dot3(left, right, ((1,), (1,)))


def mul_tn(left, right):
    return dot3(left, right, ((0,), (0,)))


def inverse_factors(grams, scratch):
    size = grams[0].shape[0]
    panels = size // ROWS8
    lane = lax.broadcasted_iota(jnp.int32, (ROWS8, size), 1)
    sub = lax.broadcasted_iota(jnp.int32, (ROWS8, size), 0)
    states = [[gram[p * ROWS8 : (p + 1) * ROWS8] for p in range(panels)] for gram in grams]
    done = [[] for _ in grams]

    def columns(block, start):
        return [
            jnp.broadcast_to(block[:, start + col : start + col + 1], (ROWS8, size))
            for col in range(ROWS8)
        ]

    for number in range(panels):
        start = number * ROWS8
        in_panel = (lane >= start) & (lane < start + ROWS8)
        unit = (lane - start == sub).astype(F32)
        for which, rows in enumerate(states):
            panel = rows[number]
            entry = {}
            slot = scratch.at[which, number % 2]
            for col, column in enumerate(columns(panel, start)):
                slot[col] = column
                for row in range(col, ROWS8):
                    entry[row, col] = jnp.broadcast_to(slot[col, row : row + 1], (ROWS8, size))
            slot[ROWS8] = jnp.where(in_panel, unit, panel)
            lines = [
                jnp.broadcast_to(slot[ROWS8, row : row + 1], (ROWS8, size)) for row in range(ROWS8)
            ]
            last = number + 1 == panels
            if not last:
                below = columns(rows[number + 1], start)
                later = jnp.where(in_panel, 0.0, rows[number + 1])
            for k in range(ROWS8):
                scale = lax.rsqrt(entry[k, k])
                lines[k] = lines[k] * scale
                for row in range(k + 1, ROWS8):
                    entry[row, k] = entry[row, k] * scale
                if not last:
                    below[k] = below[k] * scale
                    later = later - below[k] * lines[k]
                for row in range(k + 1, ROWS8):
                    factor = entry[row, k]
                    lines[row] = lines[row] - factor * lines[k]
                    if not last:
                        below[row] = below[row] - factor * below[k]
                    for col in range(k + 1, row + 1):
                        entry[row, col] = entry[row, col] - factor * entry[col, k]
            solved = lines[0]
            for k in range(1, ROWS8):
                solved = jnp.where(sub == k, lines[k], solved)
            done[which].append(jnp.where(lane < start + ROWS8, solved, 0.0))
            if not last:
                rows[number + 1] = later
            after = (number + 2) * ROWS8
            if after < size:
                high, low = split(solved)
                high_f, low_f = high.astype(F32), low.astype(F32)
                zero = jnp.zeros_like(high_f)
                left = jnp.concatenate([high_f, low_f, high_f, zero], axis=0).astype(BF16)
                right = jnp.concatenate([high_f, high_f, low_f, zero], axis=0).astype(BF16)
                update = lax.dot_general(
                    left, right, (((0,), (0,)), ((), ())), preferred_element_type=F32
                )[after:]
                for p in range(number + 2, panels):
                    begin = p * ROWS8 - after
                    rows[p] = jnp.where(in_panel, 0.0, rows[p]) - update[begin : begin + ROWS8]
    return [jnp.concatenate(rows, axis=0) for rows in done]


def gather_kernel(count, own_ref, table_ref, send_sem, recv_sem, local_sem):
    me = lax.axis_index("sub")
    barrier = pltpu.get_barrier_semaphore()

    def greet(step, carry):
        pl.semaphore_signal(
            barrier, inc=1, device_id={"sub": lax.rem(me + step, count)}, device_id_type=MESH
        )
        return carry

    lax.fori_loop(1, count, greet, 0)
    local = pltpu.make_async_copy(own_ref, table_ref.at[me], local_sem)
    local.start()
    pl.semaphore_wait(barrier, count - 1)

    def copy_of(step):
        return pltpu.make_async_remote_copy(
            src_ref=own_ref,
            dst_ref=table_ref.at[me],
            send_sem=send_sem.at[step],
            recv_sem=recv_sem.at[step],
            device_id={"sub": lax.rem(me + step, count)},
            device_id_type=MESH,
        )

    def start(step, carry):
        copy_of(step).start()
        return carry

    def finish(step, carry):
        copy_of(step).wait()
        return carry

    lax.fori_loop(1, count, start, 0)
    local.wait()
    lax.fori_loop(1, count, finish, 0)


def leaf_kernel(
    per_dev,
    kappa_ref,
    table_ref,
    leaf_tri_ref,
    leaf_proxy_ref,
    node_proxy_ref,
    mid_proxy_ref,
    root_proxy_ref,
    omega_ref,
    basis_ref,
    transfer_ref,
    coef_ref,
    sums_ref,
    cols_ref,
    rows_ref,
    weight_ref,
    high_ref,
    low_ref,
    high_too_ref,
    low_too_ref,
    sketch_ref,
    factor_ref,
):
    device = lax.axis_index("sub")
    leaves, leaf_rows = leaf_tri_ref.shape
    proxies = leaf_proxy_ref.shape[1]
    rank = omega_ref.shape[1]
    rows = leaves * leaf_rows

    turns = kappa_ref[0] * (0.5 / math.pi)
    soft = turns * turns * soft_sq
    per_axis = per_dev // LANES
    blocks = table_ref.shape[0] * ROWS8
    pieces = []
    for tile in range(table_ref.shape[1] // ROWS8):
        turned = table_ref[:, tile * ROWS8 : (tile + 1) * ROWS8, :].reshape(blocks, LANES).T
        first = turned.astype(BF16)
        left = turned - first.astype(F32)
        second = left.astype(BF16)
        third = (left - second.astype(F32)).astype(BF16)
        pieces.append((first, second, third))

    def centroids(index):
        width = index.shape[1]
        within = index & (per_dev - 1)
        block = (index >> (per_dev.bit_length() - 1)) * ROWS8 + (within >> 7)
        place = index & (LANES - 1)
        block_row = lax.broadcasted_iota(jnp.int32, (blocks, width), 0)
        hot = {
            offset: jnp.where(block_row == block + offset, 1.0, 0.0).astype(BF16)
            for offset in range(0, ROWS8, per_axis)
        }
        chosen = lax.broadcasted_iota(jnp.int32, (LANES, width), 0) == place
        found = []
        for axis in range(3):
            wide = None
            tile, offset = divmod(axis * per_axis, ROWS8)
            for piece in pieces[tile]:
                term = jnp.dot(piece, hot[offset], preferred_element_type=F32)
                wide = term if wide is None else wide + term
            found.append(jnp.sum(jnp.where(chosen, wide, 0.0), axis=0, keepdims=True) * turns)
        return found

    group = device // GROUP
    sets = [leaf_proxy_ref[leaf : leaf + 1, :] for leaf in range(leaves)]
    sets += [node_proxy_ref[...], mid_proxy_ref[pl.ds(group, 1), :], root_proxy_ref[...]]
    for number, index in enumerate(sets):
        found = centroids(index)
        for axis in range(3):
            cols_ref[number, axis : axis + 1, :] = found[axis]
    for leaf in range(leaves):
        found = centroids(leaf_tri_ref[leaf : leaf + 1, :] + device * per_dev)
        turned = jnp.concatenate(found + [jnp.zeros((ROWS8 - 3, leaf_rows), F32)], axis=0).T
        for axis in range(3):
            rows_ref[axis, leaf * leaf_rows : (leaf + 1) * leaf_rows, :] = jnp.broadcast_to(
                turned[:, axis : axis + 1], (leaf_rows, rows_ref.shape[2])
            )

    omega_high, omega_low = split(omega_ref[...] * turns)
    weight_ref[:, :rank] = omega_high
    weight_ref[:, rank:] = omega_low

    chunks = rows // ROW_CHUNK
    per_leaf = leaf_rows // ROW_CHUNK
    width = rows_ref.shape[2]

    def poly(coef, value):
        total = jnp.full_like(value, coef[-1])
        for number in coef[-2::-1]:
            total = total * value + number
        return total

    def sample(step, slot):
        level = step // chunks
        chunk = step % chunks
        number = jnp.where(level == 0, chunk // per_leaf, level + leaves - 1)
        base = pl.multiple_of(chunk * ROW_CHUNK, ROW_CHUNK)
        for top in range(0, ROW_CHUNK, 16):
            mine = [rows_ref[axis, pl.ds(base + top, 16), :] for axis in range(3)]
            for begin in range(0, proxies, width):
                squared = None
                for axis in range(3):
                    apart = mine[axis] - cols_ref[number, axis : axis + 1, begin : begin + width]
                    squared = apart * apart if squared is None else squared + apart * apart
                squared = squared + soft
                inverse = lax.rsqrt(squared)
                phase = squared * inverse
                phase = phase - jnp.round(phase)
                square = phase * phase
                sine = phase * poly(SIN_COEF, square)
                twice = poly(COS_COEF, square)
                imag = (sine * twice) * inverse
                real = (1.0 - sine * sine) * inverse
                for value, offset in ((real, 0), (imag, proxies)):
                    high, low = split(value)
                    high_refs[slot][top : top + 16, offset + begin : offset + begin + width] = high
                    low_refs[slot][top : top + 16, offset + begin : offset + begin + width] = low

    def multiply(step, slot):
        base = pl.multiple_of((step % chunks) * ROW_CHUNK, ROW_CHUNK)
        wide = jnp.dot(high_refs[slot][...], weight_ref[...], preferred_element_type=F32)
        fine = jnp.dot(low_refs[slot][...], weight_ref[:, :rank], preferred_element_type=F32)
        sketch_ref[step // chunks, pl.ds(base, ROW_CHUNK), :] = wide[:, :rank] + (
            wide[:, rank:] + fine
        )

    high_refs = (high_ref, high_too_ref)
    low_refs = (low_ref, low_too_ref)
    steps = 4 * chunks
    sample(0, 0)

    def pair(half, carry):
        step = 2 * half
        multiply(step, 0)
        sample(step + 1, 1)
        multiply(step + 1, 1)
        sample(step + 2, 0)
        return carry

    lax.fori_loop(0, steps // 2 - 1, pair, 0)
    multiply(steps - 2, 0)
    sample(steps - 1, 1)
    multiply(steps - 1, 1)

    own = [sketch_ref[0, leaf * leaf_rows : (leaf + 1) * leaf_rows, :] for leaf in range(leaves)]
    factors = inverse_factors([mul_tn(block, block) for block in own], factor_ref)
    upward = []
    for leaf in range(leaves):
        basis = mul_nt(own[leaf], factors[leaf])
        basis_ref[leaf] = basis
        far = jnp.concatenate(
            [sketch_ref[k, leaf * leaf_rows : (leaf + 1) * leaf_rows, :] for k in (1, 2, 3)], axis=1
        )
        upward.append(mul_tn(basis, far))
    stacked = jnp.concatenate(upward, axis=0)
    first = stacked[:, :rank]
    (factor,) = inverse_factors([mul_tn(first, first)], factor_ref)
    transfer = mul_nt(first, factor)
    transfer_ref[...] = transfer
    coefs = mul_tn(transfer, stacked[:, rank:])
    coef_ref[...] = coefs[:, :rank]
    sums = mul_tn(coefs[:, :rank], coefs)
    sums_ref[:rank] = sums[:, :rank]
    sums_ref[rank:] = sums[:, rank:]


def tree_kernel(
    mids,
    pos_ref,
    coef_ref,
    sums_ref,
    mid_ref,
    root_ref,
    part_ref,
    full_ref,
    own_ref,
    other_ref,
    part_send,
    part_recv,
    full_send,
    full_recv,
    root_send,
    root_recv,
    factor_ref,
):
    rank = coef_ref.shape[0]
    count = mids * GROUP
    me = lax.axis_index("sub")
    member = lax.rem(me, GROUP)
    first = me - member
    share = sums_ref.shape[0] // GROUP

    def sibling(step):
        return first + lax.rem(member + step, GROUP)

    def cousin(step):
        return lax.rem(me + step * GROUP, count)

    barrier = pltpu.get_barrier_semaphore()
    for step in range(1, GROUP):
        pl.semaphore_signal(
            barrier, inc=1, device_id={"sub": sibling(step)}, device_id_type=MESH
        )
    for step in range(1, mids):
        pl.semaphore_signal(barrier, inc=1, device_id={"sub": cousin(step)}, device_id_type=MESH)
    pl.semaphore_wait(barrier, GROUP - 1 + mids - 1)

    copies = []
    for step in range(1, GROUP):
        begin = pl.multiple_of(lax.rem(member + step, GROUP) * share, share)
        copy = pltpu.make_async_remote_copy(
            src_ref=sums_ref.at[pl.ds(begin, share)],
            dst_ref=part_ref.at[step],
            send_sem=part_send.at[step],
            recv_sem=part_recv.at[step],
            device_id={"sub": sibling(step)},
            device_id_type=MESH,
        )
        copy.start()
        copies.append(copy)
    begin = pl.multiple_of(member * share, share)
    total = sums_ref[pl.ds(begin, share), :]
    for step, copy in enumerate(copies, 1):
        copy.wait()
        total = total + part_ref[step]
    full_ref[pl.ds(begin, share), :] = total
    copies = []
    for step in range(1, GROUP):
        copy = pltpu.make_async_remote_copy(
            src_ref=full_ref.at[pl.ds(begin, share)],
            dst_ref=full_ref.at[pl.ds(begin, share)],
            send_sem=full_send.at[step],
            recv_sem=full_recv.at[step],
            device_id={"sub": sibling(step)},
            device_id_type=MESH,
        )
        copy.start()
        copies.append(copy)
    for copy in copies:
        copy.wait()

    (factor,) = inverse_factors([full_ref[:rank]], factor_ref)
    own = mul_nn(factor, full_ref[rank:])
    own_ref[...] = own
    copies = []
    for step in range(1, mids):
        copy = pltpu.make_async_remote_copy(
            src_ref=own_ref,
            dst_ref=other_ref.at[step],
            send_sem=root_send.at[step],
            recv_sem=root_recv.at[step],
            device_id={"sub": cousin(step)},
            device_id_type=MESH,
        )
        copy.start()
        copies.append(copy)
    mid_ref[...] = mul_nt(coef_ref[...], factor)
    gram = mul_tn(own, own)
    for step, copy in enumerate(copies, 1):
        copy.wait()
        other = other_ref[step]
        gram = gram + mul_tn(other, other)
    (factor,) = inverse_factors([gram], factor_ref)
    share_rows = rank // GROUP
    mine = jnp.zeros((share_rows, rank), F32)
    for place in range(GROUP):
        block = own[place * share_rows : (place + 1) * share_rows]
        mine = jnp.where(pos_ref[...] == place, block, mine)
    root_ref[...] = mul_nt(mine, factor)


def on_device(
    tri_xyz, leaf_tri, leaf_proxy, node_proxy, mid_proxy, root_proxy, level1_pos, kappa, omega
):
    count = lax.axis_size("sub")
    mids = count // GROUP
    per_dev = tri_xyz.shape[1]
    leaves, leaf_rows = leaf_tri.shape
    proxies = leaf_proxy.shape[1]
    rank = omega.shape[1]
    vmem = pl.BlockSpec(memory_space=pltpu.VMEM)
    smem = pl.BlockSpec(memory_space=pltpu.SMEM)
    dma = pltpu.SemaphoreType.DMA
    limit = 48 * 1024 * 1024

    own = tri_xyz.reshape(3 * per_dev // LANES, LANES)
    own = jnp.pad(own, ((0, -own.shape[0] % ROWS8), (0, 0)))
    table = pl.pallas_call(
        functools.partial(gather_kernel, count),
        out_shape=jax.ShapeDtypeStruct((count,) + own.shape, F32),
        in_specs=[vmem],
        out_specs=vmem,
        scratch_shapes=[dma((count,)), dma((count,)), dma],
        compiler_params=pltpu.CompilerParams(
            collective_id=0, has_side_effects=True, vmem_limit_bytes=limit
        ),
        name="gather_centroids",
    )(own)

    basis, transfer, coef, sums = pl.pallas_call(
        functools.partial(leaf_kernel, per_dev),
        out_shape=(
            jax.ShapeDtypeStruct((leaves, leaf_rows, rank), F32),
            jax.ShapeDtypeStruct((leaves * rank, rank), F32),
            jax.ShapeDtypeStruct((rank, rank), F32),
            jax.ShapeDtypeStruct((2 * rank, rank), F32),
        ),
        in_specs=[smem] + [vmem] * 7,
        out_specs=(vmem,) * 4,
        scratch_shapes=[
            pltpu.VMEM((leaves + 3, ROWS8, proxies), F32),
            pltpu.VMEM((3, leaves * leaf_rows, 2 * LANES), F32),
            pltpu.VMEM((2 * proxies, 2 * rank), BF16),
            pltpu.VMEM((ROW_CHUNK, 2 * proxies), BF16),
            pltpu.VMEM((ROW_CHUNK, 2 * proxies), BF16),
            pltpu.VMEM((ROW_CHUNK, 2 * proxies), BF16),
            pltpu.VMEM((ROW_CHUNK, 2 * proxies), BF16),
            pltpu.VMEM((4, leaves * leaf_rows, rank), F32),
            pltpu.VMEM((leaves, 2, ROWS8 + 1, ROWS8, rank), F32),
        ],
        compiler_params=pltpu.CompilerParams(vmem_limit_bytes=limit),
        name="leaf_and_node",
    )(kappa, table, leaf_tri, leaf_proxy, node_proxy, mid_proxy, root_proxy[None], omega)

    share = 2 * rank // GROUP
    mid, root = pl.pallas_call(
        functools.partial(tree_kernel, mids),
        out_shape=(
            jax.ShapeDtypeStruct((rank, rank), F32),
            jax.ShapeDtypeStruct((rank // GROUP, rank), F32),
        ),
        in_specs=[vmem, vmem, vmem],
        out_specs=(vmem, vmem),
        scratch_shapes=[
            pltpu.VMEM((GROUP, share, rank), F32),
            pltpu.VMEM((2 * rank, rank), F32),
            pltpu.VMEM((rank, rank), F32),
            pltpu.VMEM((mids, rank, rank), F32),
            dma((GROUP,)),
            dma((GROUP,)),
            dma((GROUP,)),
            dma((GROUP,)),
            dma((mids,)),
            dma((mids,)),
            pltpu.VMEM((1, 2, ROWS8 + 1, ROWS8, rank), F32),
        ],
        compiler_params=pltpu.CompilerParams(
            collective_id=1, has_side_effects=True, vmem_limit_bytes=limit
        ),
        name="mid_and_root",
    )(jnp.broadcast_to(level1_pos[0], (rank // GROUP, rank)), coef, sums)
    return (basis, transfer[None], mid[None], root[None])


def solution(mesh):
    in_specs = (
        P(None, "sub"),
        P("sub", None),
        P("sub", None),
        P("sub", None),
        P(),
        P(),
        P("sub"),
        P("freq"),
        P(),
    )
    out_specs = (
        P(("freq", "sub"), None, None),
        P(("freq", "sub"), None, None),
        P(("freq", "sub"), None, None),
        P(("freq", "sub"), None, None),
    )
    return jax.shard_map(
        on_device, mesh=mesh, in_specs=in_specs, out_specs=out_specs, check_vma=False
    )
```
